1024 devices in a mesh: expert: 64 (over z_lo, x), fsdp: 16 (over z_hi, y, core).
Axes of the slice: x: 4, y: 4, z: 32 (z_hi: 2, z_lo: 16; z = z_hi * 16 + z_lo), core: 2. Of those that a mesh axis runs over, the one named last changes fastest.
Arguments:
- tokens: bfloat16 [16384, 7168], P('expert', 'fsdp'), may hold values from -6 to 6
- output_grad: bfloat16 [16384, 7168], P('expert', 'fsdp'), may hold values from -6 to 6
- route_weight: float32 [16384, 8], P('expert'), may hold values from 0.05 to 0.5
- expert_ids: int32 [16384, 8], P('expert'), may hold values from 0 to 255, all different within a row; in each aligned block of 256 rows (0 to 255, 256 to 511, ...) at most 12 rows name the same one
- gate_weight: bfloat16 [64, 7168, 512], P('expert', 'fsdp'), may hold values from -0.0625 to 0.0625
- up_weight: bfloat16 [64, 7168, 512], P('expert', 'fsdp'), may hold values from -0.0625 to 0.0625
- down_weight: bfloat16 [64, 512, 7168], P('expert', None, 'fsdp'), may hold values from -0.1875 to 0.1875
Outputs:
- token_grad: bfloat16 [16384, 7168], P('expert', 'fsdp')
- gate_grad: bfloat16 [64, 7168, 512], P('expert', 'fsdp')
- up_grad: bfloat16 [64, 7168, 512], P('expert', 'fsdp')
- down_grad: bfloat16 [64, 512, 7168], P('expert', None, 'fsdp')
The draws below stay inside these ranges and needn't reach their ends.
Inputs may be any that keep to these rules, and one draw needn't show every extreme that they name: `expert_ids`: in each block of 256 rows (the tokens held by one position along `expert` (one block of 256 consecutive rows)) no expert is named by more than 12 rows, a bound that some block reaches.
All inputs are finite; a program needn't handle non-finite values.
Results may differ from the reference program's by a relative error of at most 0.025.
Values may be sent and summed in bfloat16 or wider, within the bound.
A program may use at most 32 MiB of HBM per device.

```python
import math
import jax
import jax.numpy as jnp
import numpy as np
from jax import lax

D = 7168
FF = 1024
EXPERTS = 256
TOPK = 8
TOK_DEV = 256
HALF = 512
CAP = 12
GROUP = 32
TOKENS = 16384
N_EXPERT = 64
N_FSDP = 16


def levels(key, dims, split, low, high):
    gain = 1.0
    for dim, shards_of in split:
        heights = jax.random.uniform(jax.random.fold_in(jax.random.fold_in(key, 6), dim), (shards_of,), jnp.float32, low / len(split), high / len(split))
        gain = gain * jnp.repeat(jnp.exp(heights), dims[dim] // shards_of).reshape((-1,) + (1,) * (len(dims) - 1 - dim))
    return gain


def deal_out(own_key, own, number, rows, amount, top, reach, lean):
    ranking = jax.random.permutation(own_key, amount)
    heavy_load, common = shares(amount, rows * top, reach, lean, True), shares(amount, rows * top, reach, lean, False)
    places = jnp.arange(amount)

    def named(tallies, offset_by):
        used = int((tallies > 0).sum())
        fixed = max(1, used // 4)
        passed = fixed + (places - fixed + offset_by * (used - fixed)) % max(1, amount - fixed)
        return jnp.zeros((amount,), jnp.int32).at[ranking[jnp.where(places < fixed, places, passed)]].set(jnp.asarray(tallies, jnp.int32))

    tallies = jnp.where(number % 4 == 0, named(heavy_load, number // 4), named(common, number - number // 4 - 1))
    mixed = jax.random.permutation(jax.random.fold_in(own, 3), amount)
    giver, taker = mixed[0:amount // 2 * 2:2], mixed[1:amount // 2 * 2:2]
    room = jnp.minimum(tallies[giver] - 1, reach - tallies[taker]) // 2
    room = jnp.where((giver == ranking[0]) | (taker == ranking[0]) | (tallies[taker] == 0), 0, jnp.maximum(room, 0))
    passed = jax.random.randint(jax.random.fold_in(own, 4), (amount // 2,), 0, 1 << 20) % (room + 1)
    tallies = tallies.at[giver].add(-passed).at[taker].add(passed)
    items = jnp.searchsorted(jnp.cumsum(tallies), jnp.arange(rows * top), side="right").astype(jnp.int32)
    table = items.reshape(top, rows).T
    table = table[jax.random.permutation(jax.random.fold_in(own, 1), rows)]
    offset_by = jax.random.randint(jax.random.fold_in(own, 2), (rows, 1), 0, top)
    return jnp.take_along_axis(table, (jnp.arange(top)[None, :] + offset_by) % top, axis=1)


def shares(amount, total, most, slope, full):
    portions = [(1 << 20) // math.isqrt(rank ** slope) + 1 for rank in range(1, amount + 1)]
    largest = most if full else min(most, max(-(-total // amount), total * portions[0] // sum(portions)))
    least = 1 if total - largest >= amount - 1 else 0
    holding, surplus = [largest] + [least] * (amount - 1), total - largest - least * (amount - 1)
    while surplus > 0:
        movable = [i for i in range(1, amount) if holding[i] < largest] or [i for i in range(1, amount) if holding[i] < most]
        mass, left = sum([portions[i] for i in movable]), surplus
        for i in movable:
            extra = min(most - holding[i], max(1, left * portions[i] // mass), surplus)
            holding[i] = holding[i] + extra
            surplus = surplus - extra
    return np.array(holding)


def noise(rng, dims, spread, bound, shards=(), kind=jnp.bfloat16):
    array = jax.random.normal(rng, dims, jnp.float32) * spread
    if len(shards) > 0:
        array = levels(rng, dims, shards, -0.22, 0.18) * array
    return jnp.clip(array, min=-bound, max=bound).astype(kind)


def setup_inputs(seed: int = 0) -> dict:
    splits = jax.random.split(jax.random.key(seed), 8)
    tokens = noise(splits[0], (TOKENS, D), 1.0, 6.0, ((0, 64), (1, 16)))
    output_grad = noise(splits[1], (TOKENS, D), 1.0, 6.0, ((0, 64), (1, 16)))
    route_weight = jnp.clip(jnp.exp(math.log(0.5) - 2.3025851 * jax.random.uniform(splits[2], (TOKENS, TOPK), jnp.float32) ** levels(splits[2], (TOKENS, TOPK), ((0, 64),), -0.2, 0.2)), 0.05, 0.5)
    expert_ids_keys = jax.random.split(jax.random.fold_in(splits[3], 1), TOKENS // TOK_DEV)
    expert_ids_turns = jax.random.permutation(jax.random.fold_in(splits[3], 3), TOKENS // TOK_DEV)
    expert_ids = jax.vmap(lambda own, number: deal_out(jax.random.fold_in(splits[3], 2), own, number, TOK_DEV, EXPERTS, TOPK, CAP, 2))(expert_ids_keys, expert_ids_turns).reshape((TOKENS, TOPK))
    gate_weight = noise(splits[4], (N_EXPERT, D, HALF), D ** -0.5, 0.0625, ((0, 64), (1, 16)))
    up_weight = noise(splits[5], (N_EXPERT, D, HALF), D ** -0.5, 0.0625, ((0, 64), (1, 16)))
    down_weight = noise(splits[6], (N_EXPERT, HALF, D), FF ** -0.5, 0.1875, ((0, 64), (2, 16)))
    return dict(tokens=tokens, output_grad=output_grad, route_weight=route_weight, expert_ids=expert_ids, gate_weight=gate_weight, up_weight=up_weight, down_weight=down_weight)


def block_sum(terms):
    rounded = lax.optimization_barrier(terms.astype(jnp.bfloat16))
    return jnp.sum(rounded.astype(jnp.float32), axis=0)


def expert_pass(rows, grads, gate_w, up_w, down_w):
    slot_count = rows.shape[0]
    hidden_width = gate_w.shape[1]
    slab_width = D // N_FSDP
    row_blocks = rows.astype(jnp.float32).reshape(slot_count, N_FSDP, slab_width)
    grad_blocks = grads.astype(jnp.float32).reshape(slot_count, N_FSDP, slab_width)
    gate_blocks = gate_w.astype(jnp.float32).reshape(N_FSDP, slab_width, hidden_width)
    up_blocks = up_w.astype(jnp.float32).reshape(N_FSDP, slab_width, hidden_width)
    down_blocks = down_w.astype(jnp.float32).reshape(hidden_width, N_FSDP, slab_width)
    highest = lax.Precision.HIGHEST
    gate = block_sum(jnp.einsum("rbd,bdf->brf", row_blocks, gate_blocks, precision=highest))
    up_value = block_sum(jnp.einsum("rbd,bdf->brf", row_blocks, up_blocks, precision=highest))
    hidden_grad = block_sum(jnp.einsum("rbd,fbd->brf", grad_blocks, down_blocks, precision=highest))
    sigmoid_gate = jax.nn.sigmoid(gate)
    activation = (gate * sigmoid_gate * up_value).astype(jnp.bfloat16)
    gate_delta = (hidden_grad * up_value * sigmoid_gate * (1.0 + gate * (1.0 - sigmoid_gate))).astype(jnp.bfloat16)
    up_delta = (hidden_grad * gate * sigmoid_gate).astype(jnp.bfloat16)
    down_grad = jnp.dot(activation.T, grads, preferred_element_type=jnp.float32).astype(jnp.bfloat16)
    gate_grad = jnp.dot(rows.T, gate_delta, preferred_element_type=jnp.float32).astype(jnp.bfloat16)
    up_grad = jnp.dot(rows.T, up_delta, preferred_element_type=jnp.float32).astype(jnp.bfloat16)
    back_rows = jnp.dot(gate_delta, gate_w.T, preferred_element_type=jnp.float32)
    back_rows = back_rows + jnp.dot(up_delta, up_w.T, preferred_element_type=jnp.float32)
    return back_rows.astype(jnp.bfloat16), gate_grad, up_grad, down_grad


def reference(tokens, output_grad, route_weight, expert_ids, gate_weight, up_weight, down_weight):
    slot_count = N_EXPERT * CAP
    in_window = expert_ids < GROUP
    expert_hits = (expert_ids[:, :, None] == jnp.arange(GROUP, dtype=jnp.int32)[None, None, :]).astype(jnp.int32)
    blocked = expert_hits.reshape(N_EXPERT, TOK_DEV * TOPK, GROUP)
    earlier = jnp.cumsum(blocked, axis=1) - blocked
    slot_rank = jnp.sum(earlier * blocked, axis=2).reshape(TOKENS, TOPK).astype(jnp.int32)
    source = (jnp.arange(TOKENS, dtype=jnp.int32) // TOK_DEV)[:, None]
    slot_index = (source * CAP + slot_rank).astype(jnp.int32)
    target = jnp.where(in_window, expert_ids, GROUP).astype(jnp.int32)
    token_index = jnp.broadcast_to(jnp.arange(TOKENS, dtype=jnp.int32)[:, None], (TOKENS, TOPK))
    table = jnp.full((GROUP, slot_count), TOKENS, jnp.int32).at[target, slot_index].set(token_index, mode="drop")
    slot_weight = jnp.zeros((GROUP, slot_count), jnp.float32).at[target, slot_index].set(route_weight, mode="drop")
    table_pairs = jnp.repeat(table, 2, axis=0)
    weight_pairs = jnp.repeat(slot_weight, 2, axis=0)
    padded_tokens = jnp.concatenate([tokens, jnp.zeros((1, D), jnp.bfloat16)], axis=0)
    padded_grads = jnp.concatenate([output_grad, jnp.zeros((1, D), jnp.bfloat16)], axis=0)

    def per_entry(total, inputs):
        rows_index, row_weight, gate_w, up_w, down_w = inputs
        rows = padded_tokens[rows_index]
        grads = (row_weight[:, None] * padded_grads[rows_index].astype(jnp.float32)).astype(jnp.bfloat16)
        back_rows, gate_grad, up_grad, down_grad = expert_pass(rows, grads, gate_w, up_w, down_w)
        total = total.at[rows_index].add(back_rows.astype(jnp.float32))
        return total, (gate_grad, up_grad, down_grad)

    start_total = jnp.zeros((TOKENS + 1, D), jnp.float32)
    total, grads_out = lax.scan(per_entry, start_total, (table_pairs, weight_pairs, gate_weight, up_weight, down_weight))
    gate_grad, up_grad, down_grad = grads_out
    return total[:TOKENS].astype(jnp.bfloat16), gate_grad, up_grad, down_grad
```

```python
import jax
import jax.numpy as jnp
from jax import lax
from jax.experimental import pallas as pl
from jax.experimental.pallas import tpu as pltpu
from jax.sharding import PartitionSpec as P

MESH = pl.DeviceIdType.MESH
BF = jnp.bfloat16
F32 = jnp.float32
CAP = 12
NX = 4
NY = 4
CHUNKS = 4

NN = (((1,), (0,)), ((), ()))
NT = (((1,), (1,)), ((), ()))
TN = (((0,), (0,)), ((), ()))


def dot(a, b, dims=NN):
    return lax.dot_general(a, b, dims, preferred_element_type=F32)


def iota(shape, dim):
    return lax.broadcasted_iota(jnp.int32, shape, dim)


def make_kernel(nz, width):
    slots = 2 * CAP
    group = nz // CHUNKS
    span = group * CAP
    rows = NX * span
    low = 2 * width - 512

    def kernel(
        ids, rw, xg, w3, wd3,
        token_grad, gate_grad, up_grad, down_grad,
        placing, send, zrecv, xsend, held, part, crecv, ysend, yrecv, zsend, zhrecv,
        hid, back, bxrecv, zret, ret,
        za_s, za_r, xa_s, xa_r, ca_s, ca_r, ya_s, ya_r, zh_s, zh_r,
        yb_s, yb_r, cb_s, cb_r, xb_s, xb_r, zb_s, zb_r,
    ):
        ei, fi = lax.axis_index("expert"), lax.axis_index("fsdp")
        zl, x = ei // NX, ei % NX
        zh, y, core = fi // (2 * NY), (fi // 2) % NY, fi % 2

        def at_z(k):
            return (lax.rem(zl + k, nz) * NX + x, fi)

        def at_x(k):
            return (zl * NX + lax.rem(x + k, NX), fi)

        def at_y(k):
            return (ei, zh * 2 * NY + lax.rem(y + k, NY) * 2 + core)

        sibling = (ei, fi + 1 - 2 * core)
        across = (ei, lax.rem(fi + 2 * NY, 4 * NY))

        barrier = pltpu.get_barrier_semaphore()
        others = [at_z(k) for k in range(1, nz)] + [at_x(k) for k in range(1, NX)]
        others += [at_y(k) for k in range(1, NY)] + [sibling, across]
        for other in others:
            pl.semaphore_signal(barrier, inc=1, device_id=other, device_id_type=MESH)

        sent = []

        def copy(src, dst, s, r, to):
            c = pltpu.make_async_remote_copy(
                src_ref=src, dst_ref=dst, send_sem=s, recv_sem=r, device_id=to, device_id_type=MESH
            )
            c.start()
            sent.append(c)
            return c

        n_exp, n_tok = 2 * nz, xg.shape[0]
        n_slot = n_exp * CAP
        names = iota((n_exp, n_tok), 0)
        hits = jnp.zeros((n_exp, n_tok), F32)
        gains = jnp.zeros((n_exp, n_tok), F32)
        for k in range(ids.shape[0]):
            same = ids[k : k + 1, :] == names
            hits = hits + jnp.where(same, 1.0, 0.0)
            gains = gains + jnp.where(same, rw[k : k + 1, :], 0.0)
        before = jnp.where(iota((n_tok, n_tok), 0) < iota((n_tok, n_tok), 1), 1.0, 0.0).astype(BF)
        rank = dot(hits.astype(BF), before)
        rank = jnp.where(hits > 0.0, rank, -1.0).astype(BF)
        first = iota((n_slot, n_exp), 1) * CAP
        row = iota((n_slot, n_exp), 0)
        owner = jnp.where((row >= first) & (row < first + CAP), 1.0, 0.0)
        slot = jnp.sum(owner * (row - first).astype(F32), axis=1, keepdims=True)
        ranks = dot(owner.astype(BF), rank)
        chosen = ranks == slot
        placing[...] = jnp.where(chosen, 1.0, 0.0).astype(BF)
        gain = lax.dot_general(
            owner, gains, NN, precision=lax.Precision.HIGHEST, preferred_element_type=F32
        )
        gain = jnp.sum(jnp.where(chosen, gain, 0.0), axis=1, keepdims=True)
        placed = dot(placing[...], xg[...])
        scale = jnp.where(iota(placed.shape, 1) < width, 1.0, gain)
        send[...] = (placed * scale).astype(BF).reshape(send.shape)

        pl.semaphore_wait(barrier, len(others))

        za = {}
        for c in range(CHUNKS):
            for m in reversed(range(group)):
                k = c + CHUNKS * m
                if k == 0:
                    continue
                za[k] = copy(
                    send.at[lax.rem(zl + nz - k, nz)], zrecv.at[c * group + m],
                    za_s.at[k], za_r.at[k], at_z(nz - k),
                )
        zrecv[0] = send[zl]

        wide = group * slots
        to, fro = iota((wide, wide), 0), iota((wide, wide), 1)
        half = jnp.where(to >= span, 1, 0)
        rest = to - half * span
        shuffle = jnp.zeros((wide, wide), F32)
        for m in range(group):
            inside = (rest >= m * CAP) & (rest < (m + 1) * CAP)
            shuffle = shuffle + jnp.where(
                inside & (fro == rest - m * CAP + m * slots + half * CAP), 1.0, 0.0
            )
        shuffle = shuffle.astype(BF)

        def products(c):
            for m in range(group):
                if c + CHUNKS * m:
                    za[c + CHUNKS * m].wait_recv()
            slabs = zrecv[c * group : (c + 1) * group].reshape(wide, 2 * width)
            xsend[c] = dot(shuffle, slabs).astype(BF).reshape(2, span, 2 * width)
            xa = [
                copy(
                    xsend.at[c, lax.rem(x + j, NX) // 2], held.at[c, j],
                    xa_s.at[c, j], xa_r.at[c, j], at_x(j),
                )
                for j in range(1, NX)
            ]
            held[c, 0] = xsend[c, x // 2]
            for cp in xa:
                cp.wait_recv()
            mine = held[c].reshape(rows, 2 * width)

            def half_product(h):
                part[c, h, :, 0:512] = dot(mine[:, 0:512], w3[h]).astype(BF)
                part[c, h, :, 512:768] = dot(mine[:, low:], wd3[h], NT).astype(BF)

            half_product(1 - core)
            ca = copy(part.at[c, 1 - core], crecv.at[c], ca_s.at[c], ca_r.at[c], sibling)
            half_product(core)
            ca.wait_recv()
            both = part[c, core].astype(F32) + crecv[c].astype(F32)
            ysend[c] = both.astype(BF).reshape(NY, span, 768)
            ya = [
                copy(
                    ysend.at[c, lax.rem(y + j, NY)], yrecv.at[c, j - 1],
                    ya_s.at[c, j], ya_r.at[c, j], at_y(j),
                )
                for j in range(1, NY)
            ]
            total = ysend[c, y].astype(F32)
            for j in range(1, NY):
                ya[j - 1].wait_recv()
                total = total + yrecv[c, j - 1].astype(F32)
            zsend[c] = total.astype(BF)
            return copy(zsend.at[c], zhrecv.at[c], zh_s.at[c], zh_r.at[c], across)

        def gradients(c, zh_copy):
            zh_copy.wait_recv()
            total = zsend[c].astype(F32) + zhrecv[c].astype(F32)
            gate, up, hgrad = total[:, 0:256], total[:, 256:512], total[:, 512:768]
            sig = 1.0 / (1.0 + jnp.exp(-gate))
            hid[c, core, y, :, 0:256] = (gate * sig * up).astype(BF)
            hid[c, core, y, :, 256:512] = (hgrad * up * sig * (1.0 + gate * (1.0 - sig))).astype(BF)
            hid[c, core, y, :, 512:768] = (hgrad * gate * sig).astype(BF)
            yb = [
                copy(
                    hid.at[c, core, y], hid.at[c, core, y],
                    yb_s.at[c, j], yb_r.at[c, j], at_y(j),
                )
                for j in range(1, NY)
            ]
            for cp in yb:
                cp.wait_recv()
            cb = copy(hid.at[c, core], hid.at[c, core], cb_s.at[c], cb_r.at[c], sibling)
            own = dot(hid[c, core, :, :, 256:768].reshape(rows, 512), w3[core], NT)
            cb.wait_recv()
            own = own + dot(hid[c, 1 - core, :, :, 256:768].reshape(rows, 512), w3[1 - core], NT)
            back[c] = own[:, 0:width].astype(BF).reshape(NX, span, width)
            return [
                copy(
                    back.at[c, j], bxrecv.at[c, j], xb_s.at[c, j], xb_r.at[c, j], at_x(NX - j)
                )
                for j in range(1, NX)
            ]

        def give_back(c, xb):
            bxrecv[c, 0] = back[c, 0]
            for cp in xb:
                cp.wait_recv()
            pair = []
            for e in range(2):
                one = bxrecv[c, lax.rem(2 * e + NX - x, NX)].astype(F32)
                two = bxrecv[c, lax.rem(2 * e + 1 + NX - x, NX)].astype(F32)
                pair.append((one + two).astype(BF))
            slabs = dot(shuffle, jnp.concatenate(pair, axis=0), TN).astype(BF)
            zret[c] = slabs.reshape(group, slots, width)
            out = []
            for m in reversed(range(group)):
                k = c + CHUNKS * m
                if k == 0:
                    ret[zl] = zret[0, 0]
                    continue
                out.append(
                    copy(zret.at[c, m], ret.at[zl], zb_s.at[k], zb_r.at[k], at_z(k))
                )
            return out

        zb = []
        across_copies = [products(c) for c in range(CHUNKS)]
        for c in range(CHUNKS):
            zb += give_back(c, gradients(c, across_copies[c]))

        rows_all = held[...].reshape(CHUNKS * rows, 2 * width)
        for h in range(2):
            grads = hid[:, h, :, :, :].reshape(CHUNKS * rows, 768)
            gu = dot(rows_all[:, 0:512], grads[:, 256:768], TN).astype(BF)
            gate_grad[:, 256 * h : 256 * h + 256] = gu[0:width, 0:256]
            up_grad[:, 256 * h : 256 * h + 256] = gu[0:width, 256:512]
            down_grad[256 * h : 256 * h + 256, :] = dot(grads[:, 0:256], rows_all[:, low:], TN).astype(BF)

        for cp in zb:
            cp.wait_recv()
        token_grad[...] = dot(placing[...], ret[...].reshape(n_slot, width), TN).astype(BF)
        for cp in sent:
            cp.wait_send()

    return kernel


def body(tokens, output_grad, route_weight, expert_ids, gate_weight, up_weight, down_weight):
    nz = lax.axis_size("expert") // NX
    width = tokens.shape[1]
    hidden = gate_weight.shape[2]
    group = nz // CHUNKS
    span = group * CAP
    rows = NX * span
    n_slot = 2 * nz * CAP
    pad = 512 - width
    xg = jnp.concatenate([tokens, output_grad], axis=1)
    halves = [
        jnp.concatenate([gate_weight[0, :, h : h + 256], up_weight[0, :, h : h + 256]], axis=1)
        for h in (0, 256)
    ]
    w3 = jnp.pad(jnp.stack(halves), ((0, 0), (0, pad), (0, 0)))
    wd3 = jnp.pad(down_weight[0], ((0, 0), (pad, 0))).reshape(2, hidden // 2, 512)
    vmem = pl.BlockSpec(memory_space=pltpu.VMEM)

    def dma(*shape):
        return [pltpu.SemaphoreType.DMA(shape)] * 2

    token_grad, gate_grad, up_grad, down_grad = pl.pallas_call(
        make_kernel(nz, width),
        out_shape=(
            jax.ShapeDtypeStruct(tokens.shape, BF),
            jax.ShapeDtypeStruct((width, hidden), BF),
            jax.ShapeDtypeStruct((width, hidden), BF),
            jax.ShapeDtypeStruct((hidden, 512), BF),
        ),
        in_specs=[vmem] * 5,
        out_specs=(vmem,) * 4,
        scratch_shapes=[
            pltpu.VMEM((n_slot, tokens.shape[0]), BF),
            pltpu.VMEM((nz, 2 * CAP, 2 * width), BF),
            pltpu.VMEM((nz, 2 * CAP, 2 * width), BF),
            pltpu.VMEM((CHUNKS, 2, span, 2 * width), BF),
            pltpu.VMEM((CHUNKS, NX, span, 2 * width), BF),
            pltpu.VMEM((CHUNKS, 2, rows, 768), BF),
            pltpu.VMEM((CHUNKS, rows, 768), BF),
            pltpu.VMEM((CHUNKS, NY, span, 768), BF),
            pltpu.VMEM((CHUNKS, NY - 1, span, 768), BF),
            pltpu.VMEM((CHUNKS, span, 768), BF),
            pltpu.VMEM((CHUNKS, span, 768), BF),
            pltpu.VMEM((CHUNKS, 2, NY, span, 768), BF),
            pltpu.VMEM((CHUNKS, NX, span, width), BF),
            pltpu.VMEM((CHUNKS, NX, span, width), BF),
            pltpu.VMEM((CHUNKS, group, 2 * CAP, width), BF),
            pltpu.VMEM((nz, 2 * CAP, width), BF),
            *dma(nz), *dma(CHUNKS, NX), *dma(CHUNKS), *dma(CHUNKS, NY), *dma(CHUNKS),
            *dma(CHUNKS, NY), *dma(CHUNKS), *dma(CHUNKS, NX), *dma(nz),
        ],
        compiler_params=pltpu.CompilerParams(
            collective_id=1, has_side_effects=True, vmem_limit_bytes=56 * 2**20
        ),
        name="layer",
    )(expert_ids.T, route_weight.T, xg, w3, wd3)
    return token_grad, gate_grad[None], up_grad[None], down_grad[None, :, pad:]


def solution(mesh):
    rows, last = P("expert", "fsdp"), P("expert", None, "fsdp")
    weight = P("expert", "fsdp", None)
    return jax.shard_map(
        body,
        mesh=mesh,
        in_specs=(rows, rows, P("expert", None), P("expert", None), weight, weight, last),
        out_specs=(rows, weight, weight, last),
        check_vma=False,
    )
```

```python
import jax
import jax.numpy as jnp
from jax import lax
from jax.experimental import pallas as pl
from jax.experimental.pallas import tpu as pltpu
from jax.sharding import PartitionSpec as P

MESH = pl.DeviceIdType.MESH
BF = jnp.bfloat16
F32 = jnp.float32
CAP = 12
NX = 4
NY = 4
CHUNKS = 4
TURN = (0, 1, 2, 3)

NN = (((1,), (0,)), ((), ()))
NT = (((1,), (1,)), ((), ()))
TN = (((0,), (0,)), ((), ()))


def dot(a, b, dims=NN):
    return lax.dot_general(a, b, dims, preferred_element_type=F32)


def iota(shape, dim):
    return lax.broadcasted_iota(jnp.int32, shape, dim)


def make_kernel(nz, width):
    slots = 2 * CAP
    group = nz // CHUNKS
    span = group * CAP
    rows = NX * span
    low = 2 * width - 512

    def kernel(
        ids, rw, tokens, output_grad, gate_w, up_w, down_w,
        token_grad, gate_grad, up_grad, down_grad,
        xg, w3, wd3, placing, send, zrecv, xsend, held, part, crecv, ysend, yrecv, zsend, zhrecv,
        hid, back, bxrecv, zret, ret,
        za_s, za_r, xa_s, xa_r, ca_s, ca_r, ya_s, ya_r, zh_s, zh_r,
        yb_s, yb_r, cb_s, cb_r, xb_s, xb_r, zb_s, zb_r,
    ):
        ei, fi = lax.axis_index("expert"), lax.axis_index("fsdp")
        zl, x = ei // NX, ei % NX
        zh, y, core = fi // (2 * NY), (fi // 2) % NY, fi % 2

        def at_z(k):
            return (lax.rem(zl + k, nz) * NX + x, fi)

        def at_x(k):
            return (zl * NX + lax.rem(x + k, NX), fi)

        def at_y(k):
            return (ei, zh * 2 * NY + lax.rem(y + k, NY) * 2 + core)

        sibling = (ei, fi + 1 - 2 * core)
        across = (ei, lax.rem(fi + 2 * NY, 4 * NY))

        barrier = pltpu.get_barrier_semaphore()
        others = [at_z(k) for k in range(1, nz)] + [at_x(k) for k in range(1, NX)]
        others += [at_y(k) for k in range(1, NY)] + [sibling, across]
        for other in others:
            pl.semaphore_signal(barrier, inc=1, device_id=other, device_id_type=MESH)

        sent = []

        def copy(src, dst, s, r, to):
            c = pltpu.make_async_remote_copy(
                src_ref=src, dst_ref=dst, send_sem=s, recv_sem=r, device_id=to, device_id_type=MESH
            )
            c.start()
            sent.append(c)
            return c

        n_exp, n_tok = 2 * nz, tokens.shape[1]
        n_slot = n_exp * CAP
        names = iota((n_exp, n_tok), 0)
        hits = jnp.zeros((n_exp, n_tok), F32)
        gains = jnp.zeros((n_exp, n_tok), F32)
        for k in range(ids.shape[0]):
            same = ids[k : k + 1, :] == names
            hits = hits + jnp.where(same, 1.0, 0.0)
            gains = gains + jnp.where(same, rw[k : k + 1, :], 0.0)
        before = jnp.where(iota((n_tok, n_tok), 0) < iota((n_tok, n_tok), 1), 1.0, 0.0).astype(BF)
        rank = dot(hits.astype(BF), before)
        rank = jnp.where(hits > 0.0, rank, -1.0).astype(BF)
        first = iota((n_slot, n_exp), 1) * CAP
        row = iota((n_slot, n_exp), 0)
        owner = jnp.where((row >= first) & (row < first + CAP), 1.0, 0.0)
        slot = jnp.sum(owner * (row - first).astype(F32), axis=1, keepdims=True)
        ranks = dot(owner.astype(BF), rank)
        chosen = ranks == slot
        placing[...] = jnp.where(chosen, 1.0, 0.0).astype(BF)
        gain = lax.dot_general(
            owner, gains, NN, precision=lax.Precision.HIGHEST, preferred_element_type=F32
        )
        gain = jnp.sum(jnp.where(chosen, gain, 0.0), axis=1, keepdims=True)
        xg[0:width] = tokens[...]
        xg[width:] = output_grad[...]
        placed = dot(placing[...], xg[...], NT)
        scale = jnp.where(iota(placed.shape, 1) < width, 1.0, gain)
        send[...] = (placed * scale).astype(BF).reshape(send.shape)

        pl.semaphore_wait(barrier, len(others))

        za = {}

        def away(k):
            return min(k, nz - k)

        def dispatch(g):
            for k in sorted(range(1, nz), key=away, reverse=True):
                if k % 4 == TURN[g]:
                    za[k] = copy(
                        send.at[lax.rem(zl + nz - k, nz)], zrecv.at[k % CHUNKS * group + k // CHUNKS],
                        za_s.at[k], za_r.at[k], at_z(nz - k),
                    )

        def dispatched(g):
            for k in za:
                if k % 4 == TURN[g]:
                    za[k].wait_send()
                    sent.remove(za[k])

        zrecv[0] = send[zl]

        wide = group * slots
        to, fro = iota((wide, wide), 0), iota((wide, wide), 1)
        half = jnp.where(to >= span, 1, 0)
        rest = to - half * span
        shuffle = jnp.zeros((wide, wide), F32)
        for m in range(group):
            inside = (rest >= m * CAP) & (rest < (m + 1) * CAP)
            shuffle = shuffle + jnp.where(
                inside & (fro == rest - m * CAP + m * slots + half * CAP), 1.0, 0.0
            )
        shuffle = shuffle.astype(BF)

        xa, ca, ya, zx, yb, cb, xb, zb = {}, {}, {}, {}, {}, {}, {}, []

        def spread(c):
            for m in range(group):
                if c + CHUNKS * m:
                    za[c + CHUNKS * m].wait_recv()
            slabs = zrecv[c * group : (c + 1) * group].reshape(wide, 2 * width)
            xsend[c] = dot(shuffle, slabs).astype(BF).reshape(2, span, 2 * width)
            xa[c] = [
                copy(
                    xsend.at[c, lax.rem(x + j, NX) // 2], held.at[c, j],
                    xa_s.at[c, j], xa_r.at[c, j], at_x(j),
                )
                for j in range(1, NX)
            ]
            held[c, 0] = xsend[c, x // 2]

        def multiply(c):
            for cp in xa[c]:
                cp.wait_recv()
            mine = held[c].reshape(rows, 2 * width)

            def half_product(h):
                part[c, h, :, 0:512] = dot(mine[:, 0:512], w3[h]).astype(BF)
                part[c, h, :, 512:768] = dot(mine[:, low:], wd3[h]).astype(BF)

            half_product(1 - core)
            ca[c] = copy(part.at[c, 1 - core], crecv.at[c], ca_s.at[c], ca_r.at[c], sibling)
            half_product(core)

        def add_cores(c):
            ca[c].wait_recv()
            both = part[c, core].astype(F32) + crecv[c].astype(F32)
            ysend[c] = both.astype(BF).reshape(NY, span, 768)
            ya[c] = [
                copy(
                    ysend.at[c, lax.rem(y + j, NY)], yrecv.at[c, j - 1],
                    ya_s.at[c, j], ya_r.at[c, j], at_y(j),
                )
                for j in range(1, NY)
            ]

        def add_columns(c):
            total = ysend[c, y].astype(F32)
            for j in range(1, NY):
                ya[c][j - 1].wait_recv()
                total = total + yrecv[c, j - 1].astype(F32)
            zsend[c] = total.astype(BF)
            zx[c] = copy(zsend.at[c], zhrecv.at[c], zh_s.at[c], zh_r.at[c], across)

        def activate(c):
            zx[c].wait_recv()
            total = zsend[c].astype(F32) + zhrecv[c].astype(F32)
            gate, up, hgrad = total[:, 0:256], total[:, 256:512], total[:, 512:768]
            sig = 1.0 / (1.0 + jnp.exp(-gate))
            hid[c, core, y, :, 0:256] = (gate * sig * up).astype(BF)
            hid[c, core, y, :, 256:512] = (hgrad * up * sig * (1.0 + gate * (1.0 - sig))).astype(BF)
            hid[c, core, y, :, 512:768] = (hgrad * gate * sig).astype(BF)
            yb[c] = [
                copy(
                    hid.at[c, core, y], hid.at[c, core, y],
                    yb_s.at[c, j], yb_r.at[c, j], at_y(j),
                )
                for j in range(1, NY)
            ]

        def gather(c):
            for cp in yb[c]:
                cp.wait_recv()
            cb[c] = copy(hid.at[c, core], hid.at[c, core], cb_s.at[c], cb_r.at[c], sibling)

        def multiply_back(c):
            own = dot(hid[c, core, :, :, 256:768].reshape(rows, 512), w3[core], NT)
            cb[c].wait_recv()
            own = own + dot(hid[c, 1 - core, :, :, 256:768].reshape(rows, 512), w3[1 - core], NT)
            back[c] = own[:, 0:width].astype(BF).reshape(NX, span, width)
            xb[c] = [
                copy(
                    back.at[c, j], bxrecv.at[c, j], xb_s.at[c, j], xb_r.at[c, j], at_x(NX - j)
                )
                for j in range(1, NX)
            ]
            bxrecv[c, 0] = back[c, 0]

        def add_halves(c):
            for cp in xb[c]:
                cp.wait_recv()
            pair = []
            for e in range(2):
                one = bxrecv[c, lax.rem(2 * e + NX - x, NX)].astype(F32)
                two = bxrecv[c, lax.rem(2 * e + 1 + NX - x, NX)].astype(F32)
                pair.append((one + two).astype(BF))
            slabs = dot(shuffle, jnp.concatenate(pair, axis=0), TN).astype(BF)
            zret[c] = slabs.reshape(group, slots, width)

        def give_back(c):
            for m in reversed(range(group)):
                k = c + CHUNKS * m
                if k == 0:
                    ret[zl] = zret[0, 0]
                    continue
                zb.append(copy(zret.at[c, m], ret.at[zl], zb_s.at[k], zb_r.at[k], at_z(k)))

        def lay_weights(_):
            for h in range(2):
                w3[h, 0:width, 0:256] = gate_w[:, 256 * h : 256 * h + 256]
                w3[h, 0:width, 256:512] = up_w[:, 256 * h : 256 * h + 256]
                w3[h, width:, :] = jnp.zeros((512 - width, 512), BF)
                wd3[h, 0 : 512 - width, :] = jnp.zeros((512 - width, 256), BF)
                wd3[h, 512 - width :, :] = down_w[:, 256 * h : 256 * h + 256]

        order = (
            (dispatch, 0), (dispatch, 1), (lay_weights, 0), (dispatched, 0), (dispatch, 2),
            (spread, 0), (multiply, 0), (dispatched, 1), (dispatch, 3), (add_cores, 0),
            (spread, 1), (multiply, 1), (add_cores, 1), (spread, 2), (multiply, 2), (add_cores, 2),
            (add_columns, 0), (add_columns, 1), (add_columns, 2), (spread, 3), (multiply, 3),
            (add_cores, 3), (add_columns, 3), (activate, 0), (gather, 0), (activate, 1),
            (multiply_back, 0), (gather, 1), (add_halves, 0), (activate, 2), (multiply_back, 1),
            (give_back, 0), (gather, 2), (add_halves, 1), (activate, 3), (multiply_back, 2),
            (give_back, 1), (gather, 3), (add_halves, 2), (give_back, 2), (multiply_back, 3),
            (add_halves, 3), (give_back, 3),
        )
        for stage, chunk in order:
            stage(chunk)

        rows_all = held[...].reshape(CHUNKS * rows, 2 * width)
        for h in range(2):
            grads = hid[:, h, :, :, :].reshape(CHUNKS * rows, 768)
            gu = dot(rows_all[:, 0:512], grads[:, 256:768], TN).astype(BF)
            gate_grad[:, 256 * h : 256 * h + 256] = gu[0:width, 0:256]
            up_grad[:, 256 * h : 256 * h + 256] = gu[0:width, 256:512]
            down = dot(rows_all[:, low:], grads[:, 0:256], TN).astype(BF)
            down_grad[:, 256 * h : 256 * h + 256] = down[512 - width :, :]

        for cp in zb:
            cp.wait_recv()
        token_grad[...] = dot(ret[...].reshape(n_slot, width), placing[...], TN).astype(BF)
        for cp in sent:
            cp.wait_send()

    return kernel


def body(tokens, output_grad, route_weight, expert_ids, gate_weight, up_weight, down_weight):
    nz = lax.axis_size("expert") // NX
    width = tokens.shape[1]
    hidden = gate_weight.shape[2]
    group = nz // CHUNKS
    span = group * CAP
    rows = NX * span
    n_slot = 2 * nz * CAP
    vmem = pl.BlockSpec(memory_space=pltpu.VMEM)

    def dma(*shape):
        return [pltpu.SemaphoreType.DMA(shape)] * 2

    token_grad, gate_grad, up_grad, down_grad = pl.pallas_call(
        make_kernel(nz, width),
        out_shape=(
            jax.ShapeDtypeStruct(tokens.shape[::-1], BF),
            jax.ShapeDtypeStruct((width, hidden), BF),
            jax.ShapeDtypeStruct((width, hidden), BF),
            jax.ShapeDtypeStruct((width, hidden), BF),
        ),
        in_specs=[vmem] * 7,
        out_specs=(vmem,) * 4,
        scratch_shapes=[
            pltpu.VMEM((2 * width, tokens.shape[0]), BF),
            pltpu.VMEM((2, 512, hidden), BF),
            pltpu.VMEM((2, 512, hidden // 2), BF),
            pltpu.VMEM((n_slot, tokens.shape[0]), BF),
            pltpu.VMEM((nz, 2 * CAP, 2 * width), BF),
            pltpu.VMEM((nz, 2 * CAP, 2 * width), BF),
            pltpu.VMEM((CHUNKS, 2, span, 2 * width), BF),
            pltpu.VMEM((CHUNKS, NX, span, 2 * width), BF),
            pltpu.VMEM((CHUNKS, 2, rows, 768), BF),
            pltpu.VMEM((CHUNKS, rows, 768), BF),
            pltpu.VMEM((CHUNKS, NY, span, 768), BF),
            pltpu.VMEM((CHUNKS, NY - 1, span, 768), BF),
            pltpu.VMEM((CHUNKS, span, 768), BF),
            pltpu.VMEM((CHUNKS, span, 768), BF),
            pltpu.VMEM((CHUNKS, 2, NY, span, 768), BF),
            pltpu.VMEM((CHUNKS, NX, span, width), BF),
            pltpu.VMEM((CHUNKS, NX, span, width), BF),
            pltpu.VMEM((CHUNKS, group, 2 * CAP, width), BF),
            pltpu.VMEM((nz, 2 * CAP, width), BF),
            *dma(nz), *dma(CHUNKS, NX), *dma(CHUNKS), *dma(CHUNKS, NY), *dma(CHUNKS),
            *dma(CHUNKS, NY), *dma(CHUNKS), *dma(CHUNKS, NX), *dma(nz),
        ],
        compiler_params=pltpu.CompilerParams(
            collective_id=1, has_side_effects=True, vmem_limit_bytes=56 * 2**20
        ),
        name="layer",
    )(
        expert_ids.T, route_weight.T, tokens.T, output_grad.T,
        gate_weight[0], up_weight[0], down_weight[0].T,
    )
    return token_grad.T, gate_grad[None], up_grad[None], down_grad.T[None]


def solution(mesh):
    rows, last = P("expert", "fsdp"), P("expert", None, "fsdp")
    weight = P("expert", "fsdp", None)
    return jax.shard_map(
        body,
        mesh=mesh,
        in_specs=(rows, rows, P("expert", None), P("expert", None), weight, weight, last),
        out_specs=(rows, weight, weight, last),
        check_vma=False,
    )
```

```python
import jax
import jax.numpy as jnp
from jax import lax
from jax.experimental import pallas as pl
from jax.experimental.pallas import tpu as pltpu
from jax.sharding import PartitionSpec as P

MESH = pl.DeviceIdType.MESH
BF = jnp.bfloat16
F32 = jnp.float32
CAP = 12
NX = 4
NY = 4
CHUNKS = 4
TURN = (0, 1, 2, 3)

NN = (((1,), (0,)), ((), ()))
NT = (((1,), (1,)), ((), ()))
TN = (((0,), (0,)), ((), ()))


def dot(a, b, dims=NN):
    return lax.dot_general(a, b, dims, preferred_element_type=F32)


def iota(shape, dim):
    return lax.broadcasted_iota(jnp.int32, shape, dim)


def settle(a, b, c, d, a_out, b_out, c_out, d_out, sems):
    copies = []
    for i, (src, dst) in enumerate(((a, a_out), (b, b_out), (c, c_out), (d, d_out))):
        rows = src.shape[0] // 4
        for j in range(4):
            part = pl.ds(j * rows, rows)
            copies.append(pltpu.make_async_copy(src.at[part], dst.at[part], sems.at[i, j]))
            copies[-1].start()
    for copy in copies:
        copy.wait()


def make_kernel(nz, width):
    slots = 2 * CAP
    group = nz // CHUNKS
    span = group * CAP
    rows = NX * span
    low = 2 * width - 512

    def kernel(
        ids, rw, tokens, output_grad, gate_w, up_w, down_w,
        token_grad, gate_grad, up_grad, down_grad,
        xg, w3, wd3, placing, send, zrecv, xsend, held, part, crecv, ysend, yrecv, zsend, zhrecv,
        hid, back, bxrecv, zret, ret,
        za_s, za_r, xa_s, xa_r, ca_s, ca_r, ya_s, ya_r, zh_s, zh_r,
        yb_s, yb_r, cb_s, cb_r, xb_s, xb_r, zb_s, zb_r,
    ):
        ei, fi = lax.axis_index("expert"), lax.axis_index("fsdp")
        zl, x = ei // NX, ei % NX
        zh, y, core = fi // (2 * NY), (fi // 2) % NY, fi % 2

        def at_z(k):
            return (lax.rem(zl + k, nz) * NX + x, fi)

        def at_x(k):
            return (zl * NX + lax.rem(x + k, NX), fi)

        def at_y(k):
            return (ei, zh * 2 * NY + lax.rem(y + k, NY) * 2 + core)

        sibling = (ei, fi + 1 - 2 * core)
        across = (ei, lax.rem(fi + 2 * NY, 4 * NY))

        barrier = pltpu.get_barrier_semaphore()
        others = [at_z(k) for k in range(1, nz)] + [at_x(k) for k in range(1, NX)]
        others += [at_y(k) for k in range(1, NY)] + [sibling, across]
        for other in others:
            pl.semaphore_signal(barrier, inc=1, device_id=other, device_id_type=MESH)

        sent = []

        def copy(src, dst, s, r, to):
            c = pltpu.make_async_remote_copy(
                src_ref=src, dst_ref=dst, send_sem=s, recv_sem=r, device_id=to, device_id_type=MESH
            )
            c.start()
            sent.append(c)
            return c

        n_exp, n_tok = 2 * nz, tokens.shape[1]
        n_slot = n_exp * CAP
        names = iota((n_exp, n_tok), 0)
        hits = jnp.zeros((n_exp, n_tok), F32)
        gains = jnp.zeros((n_exp, n_tok), F32)
        for k in range(ids.shape[0]):
            same = ids[k : k + 1, :] == names
            hits = hits + jnp.where(same, 1.0, 0.0)
            gains = gains + jnp.where(same, rw[k : k + 1, :], 0.0)
        before = jnp.where(iota((n_tok, n_tok), 0) < iota((n_tok, n_tok), 1), 1.0, 0.0).astype(BF)
        rank = dot(hits.astype(BF), before)
        rank = jnp.where(hits > 0.0, rank, -1.0).astype(BF)
        first = iota((n_slot, n_exp), 1) * CAP
        row = iota((n_slot, n_exp), 0)
        owner = jnp.where((row >= first) & (row < first + CAP), 1.0, 0.0)
        slot = jnp.sum(owner * (row - first).astype(F32), axis=1, keepdims=True)
        ranks = dot(owner.astype(BF), rank)
        chosen = ranks == slot
        placing[...] = jnp.where(chosen, 1.0, 0.0).astype(BF)
        gain = lax.dot_general(
            owner, gains, NN, precision=lax.Precision.HIGHEST, preferred_element_type=F32
        )
        gain = jnp.sum(jnp.where(chosen, gain, 0.0), axis=1, keepdims=True)
        xg[0:width] = tokens[...]
        xg[width:] = output_grad[...]
        placed = dot(placing[...], xg[...], NT)
        scale = jnp.where(iota(placed.shape, 1) < width, 1.0, gain)
        send[...] = (placed * scale).astype(BF).reshape(send.shape)

        pl.semaphore_wait(barrier, len(others))

        za = {}

        def away(k):
            return min(k, nz - k)

        def dispatch(g):
            for k in sorted(range(1, nz), key=away, reverse=True):
                if k % 4 == TURN[g]:
                    za[k] = copy(
                        send.at[lax.rem(zl + nz - k, nz)], zrecv.at[k % CHUNKS * group + k // CHUNKS],
                        za_s.at[k], za_r.at[k], at_z(nz - k),
                    )

        def dispatched(g):
            for k in za:
                if k % 4 == TURN[g]:
                    za[k].wait_send()
                    sent.remove(za[k])

        zrecv[0] = send[zl]

        wide = group * slots
        to, fro = iota((wide, wide), 0), iota((wide, wide), 1)
        half = jnp.where(to >= span, 1, 0)
        rest = to - half * span
        shuffle = jnp.zeros((wide, wide), F32)
        for m in range(group):
            inside = (rest >= m * CAP) & (rest < (m + 1) * CAP)
            shuffle = shuffle + jnp.where(
                inside & (fro == rest - m * CAP + m * slots + half * CAP), 1.0, 0.0
            )
        shuffle = shuffle.astype(BF)

        xa, ca, ya, zx, yb, cb, xb, zb = {}, {}, {}, {}, {}, {}, {}, []

        def spread(c):
            for m in range(group):
                if c + CHUNKS * m:
                    za[c + CHUNKS * m].wait_recv()
            slabs = zrecv[c * group : (c + 1) * group].reshape(wide, 2 * width)
            xsend[c] = dot(shuffle, slabs).astype(BF).reshape(2, span, 2 * width)
            xa[c] = [
                copy(
                    xsend.at[c, lax.rem(x + j, NX) // 2], held.at[c, j],
                    xa_s.at[c, j], xa_r.at[c, j], at_x(j),
                )
                for j in range(1, NX)
            ]
            held[c, 0] = xsend[c, x // 2]

        def multiply(c):
            for cp in xa[c]:
                cp.wait_recv()
            mine = held[c].reshape(rows, 2 * width)

            def half_product(h):
                part[c, h, :, 0:512] = dot(mine[:, 0:512], w3[h]).astype(BF)
                part[c, h, :, 512:768] = dot(mine[:, low:], wd3[h]).astype(BF)

            half_product(1 - core)
            ca[c] = copy(part.at[c, 1 - core], crecv.at[c], ca_s.at[c], ca_r.at[c], sibling)
            half_product(core)

        def add_cores(c):
            ca[c].wait_recv()
            both = part[c, core].astype(F32) + crecv[c].astype(F32)
            ysend[c] = both.astype(BF).reshape(NY, span, 768)
            ya[c] = [
                copy(
                    ysend.at[c, lax.rem(y + j, NY)], yrecv.at[c, j - 1],
                    ya_s.at[c, j], ya_r.at[c, j], at_y(j),
                )
                for j in range(1, NY)
            ]

        def add_columns(c):
            total = ysend[c, y].astype(F32)
            for j in range(1, NY):
                ya[c][j - 1].wait_recv()
                total = total + yrecv[c, j - 1].astype(F32)
            zsend[c] = total.astype(BF)
            zx[c] = copy(zsend.at[c], zhrecv.at[c], zh_s.at[c], zh_r.at[c], across)

        def activate(c):
            zx[c].wait_recv()
            total = zsend[c].astype(F32) + zhrecv[c].astype(F32)
            gate, up, hgrad = total[:, 0:256], total[:, 256:512], total[:, 512:768]
            sig = 1.0 / (1.0 + jnp.exp(-gate))
            hid[c, core, y, :, 0:256] = (gate * sig * up).astype(BF)
            hid[c, core, y, :, 256:512] = (hgrad * up * sig * (1.0 + gate * (1.0 - sig))).astype(BF)
            hid[c, core, y, :, 512:768] = (hgrad * gate * sig).astype(BF)
            yb[c] = [
                copy(
                    hid.at[c, core, y], hid.at[c, core, y],
                    yb_s.at[c, j], yb_r.at[c, j], at_y(j),
                )
                for j in range(1, NY)
            ]

        def gather(c):
            for cp in yb[c]:
                cp.wait_recv()
            cb[c] = copy(hid.at[c, core], hid.at[c, core], cb_s.at[c], cb_r.at[c], sibling)

        def multiply_back(c):
            own = dot(hid[c, core, :, :, 256:768].reshape(rows, 512), w3[core], NT)
            cb[c].wait_recv()
            own = own + dot(hid[c, 1 - core, :, :, 256:768].reshape(rows, 512), w3[1 - core], NT)
            back[c] = own[:, 0:width].astype(BF).reshape(NX, span, width)
            xb[c] = [
                copy(
                    back.at[c, j], bxrecv.at[c, j], xb_s.at[c, j], xb_r.at[c, j], at_x(NX - j)
                )
                for j in range(1, NX)
            ]
            bxrecv[c, 0] = back[c, 0]

        def add_halves(c):
            for cp in xb[c]:
                cp.wait_recv()
            pair = []
            for e in range(2):
                one = bxrecv[c, lax.rem(2 * e + NX - x, NX)].astype(F32)
                two = bxrecv[c, lax.rem(2 * e + 1 + NX - x, NX)].astype(F32)
                pair.append((one + two).astype(BF))
            slabs = dot(shuffle, jnp.concatenate(pair, axis=0), TN).astype(BF)
            zret[c] = slabs.reshape(group, slots, width)

        def give_back(c):
            for m in reversed(range(group)):
                k = c + CHUNKS * m
                if k == 0:
                    ret[zl] = zret[0, 0]
                    continue
                zb.append(copy(zret.at[c, m], ret.at[zl], zb_s.at[k], zb_r.at[k], at_z(k)))

        def lay_weights(_):
            for h in range(2):
                w3[h, 0:width, 0:256] = gate_w[:, 256 * h : 256 * h + 256]
                w3[h, 0:width, 256:512] = up_w[:, 256 * h : 256 * h + 256]
                w3[h, width:, :] = jnp.zeros((512 - width, 512), BF)
                wd3[h, 0 : 512 - width, :] = jnp.zeros((512 - width, 256), BF)
                wd3[h, 512 - width :, :] = down_w[:, 256 * h : 256 * h + 256]

        order = (
            (dispatch, 0), (dispatch, 1), (lay_weights, 0), (dispatched, 0), (dispatch, 2),
            (spread, 0), (multiply, 0), (dispatched, 1), (dispatch, 3), (add_cores, 0),
            (spread, 1), (multiply, 1), (add_cores, 1), (spread, 2), (multiply, 2), (add_cores, 2),
            (add_columns, 0), (add_columns, 1), (add_columns, 2), (spread, 3), (multiply, 3),
            (add_cores, 3), (add_columns, 3), (activate, 0), (gather, 0), (activate, 1),
            (multiply_back, 0), (gather, 1), (add_halves, 0), (activate, 2), (multiply_back, 1),
            (give_back, 0), (gather, 2), (add_halves, 1), (activate, 3), (multiply_back, 2),
            (give_back, 1), (gather, 3), (add_halves, 2), (give_back, 2), (multiply_back, 3),
            (add_halves, 3), (give_back, 3),
        )
        for stage, chunk in order:
            stage(chunk)

        rows_all = held[...].reshape(CHUNKS * rows, 2 * width)
        for h in range(2):
            grads = hid[:, h, :, :, :].reshape(CHUNKS * rows, 768)
            gu = dot(rows_all[:, 0:512], grads[:, 256:768], TN).astype(BF)
            gate_grad[:, 256 * h : 256 * h + 256] = gu[0:width, 0:256]
            up_grad[:, 256 * h : 256 * h + 256] = gu[0:width, 256:512]
            down = dot(rows_all[:, low:], grads[:, 0:256], TN).astype(BF)
            down_grad[:, 256 * h : 256 * h + 256] = down[512 - width :, :]

        for cp in zb:
            cp.wait_recv()
        token_grad[...] = dot(ret[...].reshape(n_slot, width), placing[...], TN).astype(BF)
        for cp in sent:
            cp.wait_send()

    return kernel


def body(tokens, output_grad, route_weight, expert_ids, gate_weight, up_weight, down_weight):
    nz = lax.axis_size("expert") // NX
    width = tokens.shape[1]
    hidden = gate_weight.shape[2]
    group = nz // CHUNKS
    span = group * CAP
    rows = NX * span
    n_slot = 2 * nz * CAP
    vmem = pl.BlockSpec(memory_space=pltpu.VMEM)

    def dma(*shape):
        return [pltpu.SemaphoreType.DMA(shape)] * 2

    made = pl.pallas_call(
        make_kernel(nz, width),
        out_shape=(
            jax.ShapeDtypeStruct(tokens.shape[::-1], BF),
            jax.ShapeDtypeStruct((width, hidden), BF),
            jax.ShapeDtypeStruct((width, hidden), BF),
            jax.ShapeDtypeStruct((width, hidden), BF),
        ),
        in_specs=[vmem] * 7,
        out_specs=(vmem,) * 4,
        scratch_shapes=[
            pltpu.VMEM((2 * width, tokens.shape[0]), BF),
            pltpu.VMEM((2, 512, hidden), BF),
            pltpu.VMEM((2, 512, hidden // 2), BF),
            pltpu.VMEM((n_slot, tokens.shape[0]), BF),
            pltpu.VMEM((nz, 2 * CAP, 2 * width), BF),
            pltpu.VMEM((nz, 2 * CAP, 2 * width), BF),
            pltpu.VMEM((CHUNKS, 2, span, 2 * width), BF),
            pltpu.VMEM((CHUNKS, NX, span, 2 * width), BF),
            pltpu.VMEM((CHUNKS, 2, rows, 768), BF),
            pltpu.VMEM((CHUNKS, rows, 768), BF),
            pltpu.VMEM((CHUNKS, NY, span, 768), BF),
            pltpu.VMEM((CHUNKS, NY - 1, span, 768), BF),
            pltpu.VMEM((CHUNKS, span, 768), BF),
            pltpu.VMEM((CHUNKS, span, 768), BF),
            pltpu.VMEM((CHUNKS, 2, NY, span, 768), BF),
            pltpu.VMEM((CHUNKS, NX, span, width), BF),
            pltpu.VMEM((CHUNKS, NX, span, width), BF),
            pltpu.VMEM((CHUNKS, group, 2 * CAP, width), BF),
            pltpu.VMEM((nz, 2 * CAP, width), BF),
            *dma(nz), *dma(CHUNKS, NX), *dma(CHUNKS), *dma(CHUNKS, NY), *dma(CHUNKS),
            *dma(CHUNKS, NY), *dma(CHUNKS), *dma(CHUNKS, NX), *dma(nz),
        ],
        compiler_params=pltpu.CompilerParams(
            collective_id=1, has_side_effects=True, vmem_limit_bytes=56 * 2**20
        ),
        name="layer",
    )(
        expert_ids.T, route_weight.T, tokens.T, output_grad.T,
        gate_weight[0], up_weight[0], down_weight[0].T,
    )
    token_grad, gate_grad, up_grad, down_grad = pl.pallas_call(
        settle,
        out_shape=[jax.ShapeDtypeStruct(m.shape, m.dtype) for m in made],
        in_specs=[pl.BlockSpec(memory_space=pl.ANY)] * 4,
        out_specs=[pl.BlockSpec(memory_space=pl.ANY)] * 4,
        scratch_shapes=[pltpu.SemaphoreType.DMA((4, 4))],
        name="settle",
    )(*made)
    return token_grad.T, gate_grad[None], up_grad[None], down_grad.T[None]


def solution(mesh):
    rows, last = P("expert", "fsdp"), P("expert", None, "fsdp")
    weight = P("expert", "fsdp", None)
    return jax.shard_map(
        body,
        mesh=mesh,
        in_specs=(rows, rows, P("expert", None), P("expert", None), weight, weight, last),
        out_specs=(rows, weight, weight, last),
        check_vma=False,
    )
```

```python
import jax
import jax.numpy as jnp
from jax import lax
from jax.experimental import pallas as pl
from jax.experimental.pallas import tpu as pltpu
from jax.sharding import PartitionSpec as P

MESH = pl.DeviceIdType.MESH
BF = jnp.bfloat16
F32 = jnp.float32
CAP = 12
NX = 4
NY = 4
CHUNKS = 4
TURN = (0, 1, 2, 3)

NN = (((1,), (0,)), ((), ()))
NT = (((1,), (1,)), ((), ()))
TN = (((0,), (0,)), ((), ()))


def dot(a, b, dims=NN):
    return lax.dot_general(a, b, dims, preferred_element_type=F32)


def iota(shape, dim):
    return lax.broadcasted_iota(jnp.int32, shape, dim)


def settle(a, b, c, d, a_out, b_out, c_out, d_out):
    for src, dst in ((a, a_out), (b, b_out), (c, c_out), (d, d_out)):
        dst[...] = src[...]


def make_kernel(nz, width):
    slots = 2 * CAP
    group = nz // CHUNKS
    span = group * CAP
    rows = NX * span
    low = 2 * width - 512

    def kernel(
        ids, rw, tokens, output_grad, gate_w, up_w, down_w,
        token_grad, gate_grad, up_grad, down_grad,
        xg, w3, wd3, placing, send, zrecv, xsend, held, part, crecv, ysend, yrecv, zsend, zhrecv,
        hid, back, bxrecv, zret, ret,
        za_s, za_r, xa_s, xa_r, ca_s, ca_r, ya_s, ya_r, zh_s, zh_r,
        yb_s, yb_r, cb_s, cb_r, xb_s, xb_r, zb_s, zb_r,
    ):
        ei, fi = lax.axis_index("expert"), lax.axis_index("fsdp")
        zl, x = ei // NX, ei % NX
        zh, y, core = fi // (2 * NY), (fi // 2) % NY, fi % 2

        def at_z(k):
            return (lax.rem(zl + k, nz) * NX + x, fi)

        def at_x(k):
            return (zl * NX + lax.rem(x + k, NX), fi)

        def at_y(k):
            return (ei, zh * 2 * NY + lax.rem(y + k, NY) * 2 + core)

        sibling = (ei, fi + 1 - 2 * core)
        across = (ei, lax.rem(fi + 2 * NY, 4 * NY))

        barrier = pltpu.get_barrier_semaphore()
        others = [at_z(k) for k in range(1, nz)] + [at_x(k) for k in range(1, NX)]
        others += [at_y(k) for k in range(1, NY)] + [sibling, across]
        for other in others:
            pl.semaphore_signal(barrier, inc=1, device_id=other, device_id_type=MESH)

        sent = []

        def copy(src, dst, s, r, to):
            c = pltpu.make_async_remote_copy(
                src_ref=src, dst_ref=dst, send_sem=s, recv_sem=r, device_id=to, device_id_type=MESH
            )
            c.start()
            sent.append(c)
            return c

        n_exp, n_tok = 2 * nz, tokens.shape[1]
        n_slot = n_exp * CAP
        names = iota((n_exp, n_tok), 0)
        hits = jnp.zeros((n_exp, n_tok), F32)
        gains = jnp.zeros((n_exp, n_tok), F32)
        for k in range(ids.shape[0]):
            same = ids[k : k + 1, :] == names
            hits = hits + jnp.where(same, 1.0, 0.0)
            gains = gains + jnp.where(same, rw[k : k + 1, :], 0.0)
        before = jnp.where(iota((n_tok, n_tok), 0) < iota((n_tok, n_tok), 1), 1.0, 0.0).astype(BF)
        rank = dot(hits.astype(BF), before)
        rank = jnp.where(hits > 0.0, rank, -1.0).astype(BF)
        first = iota((n_slot, n_exp), 1) * CAP
        row = iota((n_slot, n_exp), 0)
        owner = jnp.where((row >= first) & (row < first + CAP), 1.0, 0.0)
        slot = jnp.sum(owner * (row - first).astype(F32), axis=1, keepdims=True)
        ranks = dot(owner.astype(BF), rank)
        chosen = ranks == slot
        placing[...] = jnp.where(chosen, 1.0, 0.0).astype(BF)
        gain = lax.dot_general(
            owner, gains, NN, precision=lax.Precision.HIGHEST, preferred_element_type=F32
        )
        gain = jnp.sum(jnp.where(chosen, gain, 0.0), axis=1, keepdims=True)
        xg[0:width] = tokens[...]
        xg[width:] = output_grad[...]
        placed = dot(placing[...], xg[...], NT)
        scale = jnp.where(iota(placed.shape, 1) < width, 1.0, gain)
        send[...] = (placed * scale).astype(BF).reshape(send.shape)

        pl.semaphore_wait(barrier, len(others))

        za = {}

        def away(k):
            return min(k, nz - k)

        def dispatch(g):
            for k in sorted(range(1, nz), key=away, reverse=True):
                if k % 4 == TURN[g]:
                    za[k] = copy(
                        send.at[lax.rem(zl + nz - k, nz)], zrecv.at[k % CHUNKS * group + k // CHUNKS],
                        za_s.at[k], za_r.at[k], at_z(nz - k),
                    )

        def dispatched(g):
            for k in za:
                if k % 4 == TURN[g]:
                    za[k].wait_send()
                    sent.remove(za[k])

        zrecv[0] = send[zl]

        wide = group * slots
        to, fro = iota((wide, wide), 0), iota((wide, wide), 1)
        half = jnp.where(to >= span, 1, 0)
        rest = to - half * span
        shuffle = jnp.zeros((wide, wide), F32)
        for m in range(group):
            inside = (rest >= m * CAP) & (rest < (m + 1) * CAP)
            shuffle = shuffle + jnp.where(
                inside & (fro == rest - m * CAP + m * slots + half * CAP), 1.0, 0.0
            )
        shuffle = shuffle.astype(BF)

        xa, ca, ya, zx, yb, cb, xb, zb = {}, {}, {}, {}, {}, {}, {}, []

        def spread(c):
            for m in range(group):
                if c + CHUNKS * m:
                    za[c + CHUNKS * m].wait_recv()
            slabs = zrecv[c * group : (c + 1) * group].reshape(wide, 2 * width)
            xsend[c] = dot(shuffle, slabs).astype(BF).reshape(2, span, 2 * width)
            xa[c] = [
                copy(
                    xsend.at[c, lax.rem(x + j, NX) // 2], held.at[c, j],
                    xa_s.at[c, j], xa_r.at[c, j], at_x(j),
                )
                for j in range(1, NX)
            ]
            held[c, 0] = xsend[c, x // 2]

        def multiply(c):
            for cp in xa[c]:
                cp.wait_recv()
            mine = held[c].reshape(rows, 2 * width)

            def half_product(h):
                part[c, h, :, 0:512] = dot(mine[:, 0:512], w3[h]).astype(BF)
                part[c, h, :, 512:768] = dot(mine[:, low:], wd3[h]).astype(BF)

            half_product(1 - core)
            ca[c] = copy(part.at[c, 1 - core], crecv.at[c], ca_s.at[c], ca_r.at[c], sibling)
            half_product(core)

        def add_cores(c):
            ca[c].wait_recv()
            both = part[c, core].astype(F32) + crecv[c].astype(F32)
            ysend[c] = both.astype(BF).reshape(NY, span, 768)
            ya[c] = [
                copy(
                    ysend.at[c, lax.rem(y + j, NY)], yrecv.at[c, j - 1],
                    ya_s.at[c, j], ya_r.at[c, j], at_y(j),
                )
                for j in range(1, NY)
            ]

        def add_columns(c):
            total = ysend[c, y].astype(F32)
            for j in range(1, NY):
                ya[c][j - 1].wait_recv()
                total = total + yrecv[c, j - 1].astype(F32)
            zsend[c] = total.astype(BF)
            zx[c] = copy(zsend.at[c], zhrecv.at[c], zh_s.at[c], zh_r.at[c], across)

        def activate(c):
            zx[c].wait_recv()
            total = zsend[c].astype(F32) + zhrecv[c].astype(F32)
            gate, up, hgrad = total[:, 0:256], total[:, 256:512], total[:, 512:768]
            sig = 1.0 / (1.0 + jnp.exp(-gate))
            hid[c, core, y, :, 0:256] = (gate * sig * up).astype(BF)
            hid[c, core, y, :, 256:512] = (hgrad * up * sig * (1.0 + gate * (1.0 - sig))).astype(BF)
            hid[c, core, y, :, 512:768] = (hgrad * gate * sig).astype(BF)
            yb[c] = [
                copy(
                    hid.at[c, core, y], hid.at[c, core, y],
                    yb_s.at[c, j], yb_r.at[c, j], at_y(j),
                )
                for j in range(1, NY)
            ]

        def gather(c):
            for cp in yb[c]:
                cp.wait_recv()
            cb[c] = copy(hid.at[c, core], hid.at[c, core], cb_s.at[c], cb_r.at[c], sibling)

        def multiply_back(c):
            own = dot(hid[c, core, :, :, 256:768].reshape(rows, 512), w3[core], NT)
            cb[c].wait_recv()
            own = own + dot(hid[c, 1 - core, :, :, 256:768].reshape(rows, 512), w3[1 - core], NT)
            back[c] = own[:, 0:width].astype(BF).reshape(NX, span, width)
            xb[c] = [
                copy(
                    back.at[c, j], bxrecv.at[c, j], xb_s.at[c, j], xb_r.at[c, j], at_x(NX - j)
                )
                for j in range(1, NX)
            ]
            bxrecv[c, 0] = back[c, 0]

        def add_halves(c):
            for cp in xb[c]:
                cp.wait_recv()
            pair = []
            for e in range(2):
                one = bxrecv[c, lax.rem(2 * e + NX - x, NX)].astype(F32)
                two = bxrecv[c, lax.rem(2 * e + 1 + NX - x, NX)].astype(F32)
                pair.append((one + two).astype(BF))
            slabs = dot(shuffle, jnp.concatenate(pair, axis=0), TN).astype(BF)
            zret[c] = slabs.reshape(group, slots, width)

        def give_back(c):
            for m in reversed(range(group)):
                k = c + CHUNKS * m
                if k == 0:
                    ret[zl] = zret[0, 0]
                    continue
                zb.append(copy(zret.at[c, m], ret.at[zl], zb_s.at[k], zb_r.at[k], at_z(k)))

        def lay_weights(_):
            for h in range(2):
                w3[h, 0:width, 0:256] = gate_w[:, 256 * h : 256 * h + 256]
                w3[h, 0:width, 256:512] = up_w[:, 256 * h : 256 * h + 256]
                w3[h, width:, :] = jnp.zeros((512 - width, 512), BF)
                wd3[h, 0 : 512 - width, :] = jnp.zeros((512 - width, 256), BF)
                wd3[h, 512 - width :, :] = down_w[:, 256 * h : 256 * h + 256]

        order = (
            (dispatch, 0), (dispatch, 1), (lay_weights, 0), (dispatched, 0), (dispatch, 2),
            (spread, 0), (multiply, 0), (dispatched, 1), (dispatch, 3), (add_cores, 0),
            (spread, 1), (multiply, 1), (add_cores, 1), (spread, 2), (multiply, 2), (add_cores, 2),
            (add_columns, 0), (add_columns, 1), (add_columns, 2), (spread, 3), (multiply, 3),
            (add_cores, 3), (add_columns, 3), (activate, 0), (gather, 0), (activate, 1),
            (multiply_back, 0), (gather, 1), (add_halves, 0), (activate, 2), (multiply_back, 1),
            (give_back, 0), (gather, 2), (add_halves, 1), (activate, 3), (multiply_back, 2),
            (give_back, 1), (gather, 3), (add_halves, 2), (give_back, 2), (multiply_back, 3),
            (add_halves, 3), (give_back, 3),
        )
        for stage, chunk in order:
            stage(chunk)

        rows_all = held[...].reshape(CHUNKS * rows, 2 * width)
        for h in range(2):
            grads = hid[:, h, :, :, :].reshape(CHUNKS * rows, 768)
            gu = dot(rows_all[:, 0:512], grads[:, 256:768], TN).astype(BF)
            gate_grad[:, 256 * h : 256 * h + 256] = gu[0:width, 0:256]
            up_grad[:, 256 * h : 256 * h + 256] = gu[0:width, 256:512]
            down = dot(rows_all[:, low:], grads[:, 0:256], TN).astype(BF)
            down_grad[:, 256 * h : 256 * h + 256] = down[512 - width :, :]

        for cp in zb:
            cp.wait_recv()
        token_grad[...] = dot(ret[...].reshape(n_slot, width), placing[...], TN).astype(BF)
        for cp in sent:
            cp.wait_send()

    return kernel


def body(tokens, output_grad, route_weight, expert_ids, gate_weight, up_weight, down_weight):
    nz = lax.axis_size("expert") // NX
    width = tokens.shape[1]
    hidden = gate_weight.shape[2]
    group = nz // CHUNKS
    span = group * CAP
    rows = NX * span
    n_slot = 2 * nz * CAP
    vmem = pl.BlockSpec(memory_space=pltpu.VMEM)

    def dma(*shape):
        return [pltpu.SemaphoreType.DMA(shape)] * 2

    made = pl.pallas_call(
        make_kernel(nz, width),
        out_shape=(
            jax.ShapeDtypeStruct(tokens.shape[::-1], BF),
            jax.ShapeDtypeStruct((width, hidden), BF),
            jax.ShapeDtypeStruct((width, hidden), BF),
            jax.ShapeDtypeStruct((width, hidden), BF),
        ),
        in_specs=[vmem] * 7,
        out_specs=(vmem,) * 4,
        scratch_shapes=[
            pltpu.VMEM((2 * width, tokens.shape[0]), BF),
            pltpu.VMEM((2, 512, hidden), BF),
            pltpu.VMEM((2, 512, hidden // 2), BF),
            pltpu.VMEM((n_slot, tokens.shape[0]), BF),
            pltpu.VMEM((nz, 2 * CAP, 2 * width), BF),
            pltpu.VMEM((nz, 2 * CAP, 2 * width), BF),
            pltpu.VMEM((CHUNKS, 2, span, 2 * width), BF),
            pltpu.VMEM((CHUNKS, NX, span, 2 * width), BF),
            pltpu.VMEM((CHUNKS, 2, rows, 768), BF),
            pltpu.VMEM((CHUNKS, rows, 768), BF),
            pltpu.VMEM((CHUNKS, NY, span, 768), BF),
            pltpu.VMEM((CHUNKS, NY - 1, span, 768), BF),
            pltpu.VMEM((CHUNKS, span, 768), BF),
            pltpu.VMEM((CHUNKS, span, 768), BF),
            pltpu.VMEM((CHUNKS, 2, NY, span, 768), BF),
            pltpu.VMEM((CHUNKS, NX, span, width), BF),
            pltpu.VMEM((CHUNKS, NX, span, width), BF),
            pltpu.VMEM((CHUNKS, group, 2 * CAP, width), BF),
            pltpu.VMEM((nz, 2 * CAP, width), BF),
            *dma(nz), *dma(CHUNKS, NX), *dma(CHUNKS), *dma(CHUNKS, NY), *dma(CHUNKS),
            *dma(CHUNKS, NY), *dma(CHUNKS), *dma(CHUNKS, NX), *dma(nz),
        ],
        compiler_params=pltpu.CompilerParams(
            collective_id=1, has_side_effects=True, vmem_limit_bytes=56 * 2**20
        ),
        name="layer",
    )(
        expert_ids.T, route_weight.T, tokens.T, output_grad.T,
        gate_weight[0], up_weight[0], down_weight[0].T,
    )
    token_grad, gate_grad, up_grad, down_grad = pl.pallas_call(
        settle,
        out_shape=[jax.ShapeDtypeStruct(m.shape, m.dtype) for m in made],
        in_specs=[vmem] * 4,
        out_specs=[vmem] * 4,
        name="settle",
    )(*made)
    return token_grad.T, gate_grad[None], up_grad[None], down_grad.T[None]


def solution(mesh):
    rows, last = P("expert", "fsdp"), P("expert", None, "fsdp")
    weight = P("expert", "fsdp", None)
    return jax.shard_map(
        body,
        mesh=mesh,
        in_specs=(rows, rows, P("expert", None), P("expert", None), weight, weight, last),
        out_specs=(rows, weight, weight, last),
        check_vma=False,
    )
```
